768 devices in a mesh: row: 32 (over y, z_lo), col: 24 (over z_hi, x, core).
Axes of the slice: x: 4, y: 8, z: 12 (z_hi: 3, z_lo: 4; z = z_hi * 4 + z_lo), core: 2. Of those that a mesh axis runs over, the one named last changes fastest.
Arguments:
- a_vals: bfloat16 [32, 264, 128, 128], P('row', 'col'), may hold values from -0.0625 to 0.0625
- a_row: int32 [32, 264], P('row', 'col'), may hold values from 0 to 4, as said below
- a_col: int32 [32, 264], P('row', 'col'), may hold values from 0 to 767, as said below
- group_rows: int32 [32], P('row'), may hold values from 1 to 4, 96 in all
- b_panel: bfloat16 [98304, 3072], P('row', 'col'), may hold values from -6 to 6
- c_mask: int32 [128, 24], P('row', 'col'), may hold values 0 or 1
Outputs:
- product: bfloat16 [16384, 3072], P('row', 'col')
The draws below stay inside these ranges and needn't reach their ends.
Inputs may be any that keep to these rules, and one draw needn't show every extreme that they name: `a_row`: 4 marks an empty slot; every slot from 256 on is empty; slots with equal s // 4 below that name different block rows or are empty. `a_col`: slots with equal s // 4 below 256 name the same block column k, with k // 24 == s // 8.
All inputs are finite; a program needn't handle non-finite values. No bound on the sum of `group_rows` or of `c_mask` on one device may be relied on, other than what follows from the above.
Results may differ from the reference program's by a relative error of at most 0.011.
Values may be sent and summed in bfloat16 or wider, within the bound.
A program may use at most 64 MiB of HBM per device.

```python
import math
import jax
import jax.numpy as jnp
import numpy as np
from jax import lax

BS = 128
RCAP = 4
CAPQ = 2
KB_DEV = 24
KB = 768
SLOTS = 264
TOTAL_ROWS = 96
MB = 128
NB = 24
N_ROW = 32


def draw_a_row(key, part):
    key = jax.random.fold_in(key, 11)
    first, second = jax.random.split(key)
    lists = N_ROW * CAPQ
    used = lists * RCAP
    scores = jax.random.randint(first, (N_ROW, lists, RCAP), 0, 1 << 20) * RCAP
    scores = scores + jnp.arange(RCAP, dtype=jnp.int32)[None, None, :]
    order = jnp.argsort(scores, axis=2).astype(jnp.int32)
    empty = jax.random.randint(second, (N_ROW, lists, RCAP), 0, 8) == 0
    order = jnp.where(empty, RCAP, order).reshape(N_ROW, used)
    rows = jnp.full((N_ROW, SLOTS), RCAP, jnp.int32)
    rows = rows.at[:, :used].set(order)
    rows = rows.at[0, used - 1].set(RCAP)
    return rows.astype(jnp.int32)


def draw_a_col(key, part):
    key = jax.random.fold_in(key, 23)
    first, second = jax.random.split(key)
    lists = N_ROW * CAPQ
    used = lists * RCAP
    local = jax.random.randint(first, (N_ROW, lists), 0, KB_DEV)
    local = local.at[0, 0].set(0)
    local = local.at[0, lists - 1].set(KB_DEV - 1)
    owner = jnp.arange(lists, dtype=jnp.int32)[None, :] // CAPQ
    list_cols = owner * KB_DEV + local
    spread = jnp.repeat(list_cols, RCAP, axis=1)
    spare = jax.random.randint(second, (N_ROW, SLOTS), 0, KB)
    cols = spare.at[:, :used].set(spread)
    return cols.astype(jnp.int32)


def plant(values, key, smallest, largest):
    extent = values.shape
    index_at = [jax.random.randint(jax.random.fold_in(key, axis), (), 0, extent[axis]) for axis in range(len(extent))]
    values = values.at[tuple(index_at)].set(smallest)
    longest = extent.index(max(extent))
    index_at[longest] = (index_at[longest] + 1) % extent[longest]
    return values.at[tuple(index_at)].set(largest)


def block_scale(key, extent, shards, smallest, high):
    def one(position, shards_of):
        steps = jax.random.uniform(jax.random.fold_in(jax.random.fold_in(key, 6), position), (shards_of,), jnp.float32, smallest / len(shards), high / len(shards))
        return jnp.repeat(jnp.exp(steps), extent[position] // shards_of).reshape((-1,) + (1,) * (len(extent) - position - 1))

    loudness = one(*shards[0])
    for cut in shards[1:]:
        loudness = loudness * one(*cut)
    return loudness


def length_profile(amount, total, bound, slope):
    portions = [(1 << 20) // math.isqrt(rank ** slope) + 1 for rank in range(2, amount + 1)]
    rest, given = total - bound - (amount - 1), [1] * (amount - 1)
    while rest > 0:
        free = [i for i in range(amount - 1) if given[i] < bound]
        mass, left = sum([portions[i] for i in free]), rest
        for i in free:
            more = min(bound - given[i], max(1, left * portions[i] // mass), rest)
            given[i] = given[i] + more
            rest = rest - more
    return np.array([bound] + given)


def uneven(stream_key, count, total, limit, lean):
    if count == 2:
        one = jax.random.randint(stream_key, (), max(1, total - limit), min(limit, total - 1) + 1)
        return jnp.stack([one, total - one])
    lengths = jnp.asarray(length_profile(count, total, limit, lean), jnp.int32)
    pairs = (count - 1) // 2
    source_of, taker = lengths[1:1 + 2 * pairs:2], lengths[2:2 + 2 * pairs:2]
    slack = jnp.minimum(source_of - 1, limit - taker)
    passed = jax.random.randint(jax.random.fold_in(stream_key, 1), (pairs,), 0, 1 << 20) % (slack + 1)
    lengths = lengths.at[1:1 + 2 * pairs:2].set(source_of - passed).at[2:2 + 2 * pairs:2].set(taker + passed)
    return lengths[jax.random.permutation(jax.random.fold_in(stream_key, 2), count)]


def gaussian(stream_key, extent, scale, most, cuts=(), kind=jnp.bfloat16):
    values = jax.random.normal(stream_key, extent, jnp.float32) * scale
    if len(cuts) > 0:
        values = block_scale(stream_key, extent, cuts, -0.22, 0.18) * values
    return jnp.clip(values, min=-most, max=most).astype(kind)


def setup_inputs(seed: int = 0) -> dict:
    key_list = jax.random.split(jax.random.key(seed), 7)
    return {
        "a_vals": gaussian(key_list[0], (N_ROW, SLOTS, BS, BS), (BS * CAPQ * N_ROW) ** -0.5, 0.0625, ((0, 32), (1, 24))),
        "a_row": draw_a_row(jax.random.fold_in(key_list[6], 71), 0),
        "a_col": draw_a_col(jax.random.fold_in(key_list[6], 71), 0),
        "group_rows": uneven(key_list[3], N_ROW, TOTAL_ROWS, RCAP, 2).astype(jnp.int32),
        "b_panel": gaussian(key_list[4], (KB * BS, NB * BS), 1.0, 6.0, ((0, 32), (1, 24))),
        "c_mask": plant((jax.random.randint(key_list[5], (MB, NB), 0, 4) < 3).astype(jnp.int32), jax.random.fold_in(key_list[5], 1), 0, 1),
    }


def group_rows_of(a_blocks, rows, cols, live_count, mask_rows, panel_blocks):
    lists = N_ROW * CAPQ
    used = lists * RCAP
    blocks = a_blocks[:used].reshape(lists, RCAP, BS, BS).astype(jnp.float32)
    slot_rows = rows[:used].reshape(lists, RCAP)
    list_cols = cols[:used].reshape(lists, RCAP)[:, 0]
    places = jnp.arange(RCAP, dtype=jnp.int32)
    onehot = ((slot_rows[:, :, None] == places[None, None, :]) & (slot_rows[:, :, None] < live_count)).astype(jnp.float32)
    placed = jnp.einsum("lri,lrab->liab", onehot, blocks)
    chosen = panel_blocks[list_cols].astype(jnp.float32)
    full = jnp.einsum("liab,lbn->ian", placed, chosen)
    full = full.reshape(RCAP, BS, NB, BS) * mask_rows.astype(jnp.float32)[:, None, :, None]
    return full.astype(jnp.bfloat16)


def reference(a_vals, a_row, a_col, group_rows, b_panel, c_mask):
    panel_blocks = b_panel.reshape(KB, BS, NB * BS)
    masks = c_mask.reshape(N_ROW, RCAP, NB)

    def one_group(items):
        return group_rows_of(items[0], items[1], items[2], items[3], items[4], panel_blocks)

    result = lax.map(one_group, (a_vals, a_row, a_col, group_rows, masks))
    return result.reshape(MB * BS, NB * BS)
```

```python
import jax
import jax.numpy as jnp
from jax import lax
from jax.experimental import pallas as pl
from jax.experimental.pallas import tpu as pltpu
from jax.sharding import PartitionSpec as P

BS = 128
RCAP = 4
KB_DEV = 24
PER_DEV = 11
USED = 256
N_ROW = 32
N_COL = 24
NY, NZ, NH, NX = 8, 4, 3, 4
LIST8 = 8
ZERO = 64
MESH = pl.DeviceIdType.MESH


def div(a, b):
    return lax.div(jnp.int32(a), jnp.int32(b))


def rem(a, b):
    return lax.rem(jnp.int32(a), jnp.int32(b))


def owners_in(zl, h):
    first = PER_DEV * h + rem(zl + h, NZ)
    last = jnp.minimum(PER_DEV * h + PER_DEV - 1, N_ROW - 1)
    return div(first, NZ), first + 2 * NZ <= last


def kernel(
    a_ref, row_hbm, col_hbm, live_hbm, b_hbm, mask_hbm, out_ref,
    row_ref, col_ref, live_ref, b_ref, mask_ref, l_in, a0, a1, a2, a3, bbuf, bstage, pk, ix1, ix2, sx, rbuf, rs, idxs, ostage, obuf, acc,
    s_i1, r_i1, s_i2, r_i2, l_i2, s_s1, r_s1, s_s2, r_s2, s_x, r_x, s_f, r_f, s_c, r_c,
    s_b, r_b, s_r, r_r, l_r, s_o, r_o,
):
    held = (a0, a1, a2, a3)
    r = lax.axis_index("row")
    c = lax.axis_index("col")
    y, zl = div(r, NZ), rem(r, NZ)
    h, e = div(c, 8), rem(c, 8)
    x, k = div(e, 2), rem(e, 2)
    ca, cb = div(LIST8 * r, PER_DEV), div(LIST8 * r + LIST8 - 1, PER_DEV)
    two = cb != ca
    holds = (c == ca) | (c == cb)
    slot = jnp.where(c == ca, 0, 1)
    o_lo = div(PER_DEV * c, LIST8)
    o_hi = jnp.minimum(div(PER_DEV * c + PER_DEV - 1, LIST8), N_ROW - 1)

    y0, three = owners_in(zl, h)

    def at_h(d):
        return (r, rem(h + d, NH) * 8 + e)

    def at_x(d):
        return (r, h * 8 + rem(x + d, NX) * 2 + k)

    def at_y(d):
        return (rem(y + d, NY) * NZ + zl, c)

    def at_z(z):
        return (y * NZ + z, c)

    other = (r, h * 8 + 2 * x + 1 - k)

    def remote(src, dst, s_sem, r_sem, device):
        return pltpu.make_async_remote_copy(
            src_ref=src, dst_ref=dst, send_sem=s_sem, recv_sem=r_sem,
            device_id=device, device_id_type=MESH,
        )

    loads = [
        pltpu.make_async_copy(src, dst, l_in.at[i])
        for i, (src, dst) in enumerate(
            (
                (row_hbm, row_ref), (col_hbm, col_ref), (live_hbm, live_ref),
                (b_hbm, b_ref), (mask_hbm, mask_ref),
            )
        )
    ]
    for load in loads:
        load.start()

    barrier = pltpu.get_barrier_semaphore()

    def signal(device):
        pl.semaphore_signal(barrier, inc=1, device_id=device, device_id_type=MESH)

    for d in (1, 2):
        signal(at_h(d))
    for d in (1, 3):
        signal(at_x(d))
    signal(other)
    for d in range(1, NY):
        signal(at_y(d))
    for d in range(1, NZ):
        signal(at_z(rem(zl + d, NZ)))

    def greet_s1(i, _):
        g, t = rem(i, NZ), div(i, NZ)
        o = (y0 + t) * NZ + zl
        cs = div(LIST8 * o + e, PER_DEV)
        ok = (t < 2) | three

        @pl.when(ok & ((g != zl) | (cs != c)))
        def _():
            signal((y * NZ + g, cs))

        return 0

    lax.fori_loop(0, 12, greet_s1, 0)

    @pl.when(c != ca)
    def _():
        signal((r, ca))

    @pl.when(two & (c != cb))
    def _():
        signal((r, cb))

    @pl.when(holds)
    def _():
        def greet(i, _):
            signal((rem(r + i, N_ROW), c))
            return 0

        lax.fori_loop(1, N_ROW, greet, 0)

    def is_self(j):
        s = PER_DEV * c + j
        return (rem(div(s, LIST8), NZ) == zl) & (rem(s, LIST8) == e)

    for load in loads[:3]:
        load.wait()
    rows = row_ref[...]
    rows = jnp.where(rows < live_ref[0], rows, RCAP)
    pk[...] = jnp.zeros_like(pk)
    pk[:, 0:PER_DEV] = col_ref[...] * 8 + rows
    for n in range(4):
        held[n][ZERO] = jnp.zeros((BS, BS), jnp.bfloat16)

    expect = jnp.int32(15)
    for j in range(PER_DEV):
        s = PER_DEV * c + j
        expect = expect + jnp.where((s < USED) & jnp.logical_not(is_self(j)), 1, 0)
    for t in range(3):
        expect = expect + jnp.where((o_lo + t <= o_hi) & (o_lo + t != r), 1, 0)
    expect = expect + jnp.where(holds, N_COL - 1, 0)
    pl.semaphore_wait(barrier, expect)

    def i1(t):
        o = o_lo + t
        return (
            (o <= o_hi) & (o != r),
            (o <= o_hi) & (o == r),
            remote(pk, ix1.at[r], s_i1.at[t], r_i1.at[r], (o, c)),
            pltpu.make_async_copy(pk, ix1.at[r], r_i1.at[r]),
        )

    for t in range(3):
        away, here, far, near = i1(t)
        pl.when(away)(far.start)
        pl.when(here)(near.start)

    def send_s1(n):
        zd = rem(zl + 3 - n, NZ)

        def one(j, _):
            s = PER_DEV * c + j
            e2, y2 = rem(s, LIST8), div(s, 4 * LIST8)
            ok = (s < USED) & (rem(div(s, LIST8), NZ) == zd)
            src, dst, sem = a_ref.at[j], held[n].at[e2 * 8 + y2], r_s1.at[n, y2]
            if n == 3:

                @pl.when(ok & (e2 == e))
                def _():
                    pltpu.make_async_copy(src, dst, sem).start()

                ok = ok & (e2 != e)

            @pl.when(ok)
            def _():
                remote(src, dst, s_s1.at[j], sem, (y * NZ + zd, h * 8 + e2)).start()

            return 0

        lax.fori_loop(0, PER_DEV, one, 0)

    for n in range(4):
        send_s1(n)

    def i2(cc):
        return remote(ix1, ix2.at[slot], s_i2.at[cc], r_i2.at[slot], (r, cc))

    @pl.when(holds)
    def _():
        def take(i, _):
            remote(pk, ix1.at[i], s_i1.at[0], r_i1.at[i], other).wait_recv()
            return 0

        lax.fori_loop(0, N_ROW, take, 0)
        pltpu.make_async_copy(ix1, ix2.at[slot], r_i2.at[slot]).start()

        def give(i, _):
            i2(rem(c + i, N_COL)).start()
            return 0

        lax.fori_loop(1, N_COL, give, 0)

    def s2(n, d, part):
        src = held[n].at[pl.ds(e * 8 + y0 + 2 * part, 2 - part)]
        return remote(src, src, s_s2.at[n, d - 1, part], r_s2.at[n, d - 1, part], at_h(d))

    def take_s1(n, t):
        dst = held[n].at[e * 8 + y0 + t]
        remote(dst, dst, s_s1.at[0], r_s1.at[n, y0 + t], other).wait_recv()

    def send_s2(n):
        take_s1(n, 0)
        take_s1(n, 1)
        for d in (1, 2):
            s2(n, d, 0).start()

        @pl.when(three)
        def _():
            take_s1(n, 2)
            for d in (1, 2):
                s2(n, d, 1).start()

    send_s2(0)
    send_s2(1)

    def wait_i2(i):
        remote(ix1, ix2.at[i], s_i2.at[0], r_i2.at[i], other).wait_recv()
        pltpu.make_async_copy(ix2.at[i], sx.at[i], l_i2.at[i]).start()

    wait_i2(0)
    pl.when(two)(lambda: wait_i2(1))
    pltpu.make_async_copy(ix2.at[0], sx.at[0], l_i2.at[0]).wait()
    pl.when(two)(pltpu.make_async_copy(ix2.at[1], sx.at[1], l_i2.at[1]).wait)

    def b_copy(n, d):
        return remote(bstage.at[n, d], bbuf.at[n, y], s_b.at[n, d], r_b.at[n, d], at_y(d))

    def place(o, t):
        s = LIST8 * o + t
        cs = div(s, PER_DEV)
        return jnp.where(cs == div(LIST8 * o, PER_DEV), 0, 1), s - PER_DEV * cs

    def chosen(rr, q):
        which, lane = place(r, RCAP * q)
        return jnp.clip((sx[which, rr, 0, lane] >> 3) - KB_DEV * r, 0, KB_DEV - 1)

    def send_b(n):
        g = rem(zl + 1 + n, NZ)

        def one(i, _):
            d = 1 + rem(3 * i + 3, 7)
            for q in range(2):
                bstage[n, d, q] = b_ref[chosen(rem(y + d, NY) * NZ + g, q)]
            b_copy(n, d).start()
            return 0

        lax.fori_loop(0, NY - 1, one, 0)
        for q in range(2):
            bbuf[n, y, q] = b_ref[chosen(r - zl + g, q)]

    def sent_b(n):
        def one(d, _):
            b_copy(n, d).wait_send()
            return 0

        lax.fori_loop(1, NY, one, 0)

    def r_copy(d, i):
        src = ix2.at[i, pl.ds(rem(y + d, NY) * NZ, NZ)]
        return remote(src, rbuf.at[y, i], s_r.at[d, i], r_r.at[d, i], at_y(d))

    def r_own(i):
        return pltpu.make_async_copy(ix2.at[i, pl.ds(y * NZ, NZ)], rbuf.at[y, i], r_r.at[0, i])

    def send_r():
        def one(d, _):
            r_copy(d, 0).start()
            pl.when(two)(lambda: r_copy(d, 1).start())
            return 0

        lax.fori_loop(1, NY, one, 0)
        r_own(0).start()
        pl.when(two)(lambda: r_own(1).start())

    loads[3].wait()
    send_b(0)
    send_r()
    send_b(1)
    send_b(2)

    def chunk(n, ec, lo=0, size=8):
        return held[n].at[pl.ds(ec * 8 + lo, size)]

    e_of = [rem(x + d, NX) * 2 + k for d in range(NX)]

    def x_copy(n, way):
        src = chunk(n, e)
        return remote(src, src, s_x.at[n, way], r_x.at[n, way], at_x((1, 3)[way]))

    def f_copy(n, way):
        src = chunk(n, e_of[(3, 1)[way]], 4 * way, 4)
        return remote(src, src, s_f.at[n, way], r_f.at[n, way], at_x((1, 3)[way]))

    def c_copy(n, d):
        src = chunk(n, e_of[d])
        return remote(src, src, s_c.at[n, d], r_c.at[n, d], other)

    def landed(ref, sem):
        remote(ref, ref, s_c.at[0, 0], sem, other).wait_recv()

    def own_chunk(n):
        for d in (1, 2):
            ys, three_s = owners_in(zl, rem(h + NH - d, NH))
            at = e * 8 + ys
            landed(held[n].at[pl.ds(at, 2)], r_s2.at[n, d - 1, 0])

            @pl.when(three_s)
            def _(at=at, d=d):
                landed(held[n].at[pl.ds(at + 2, 1)], r_s2.at[n, d - 1, 1])

        x_copy(n, 0).start()
        x_copy(n, 1).start()
        c_copy(n, 0).start()

    def near_chunks(n):
        for way in range(2):
            landed(chunk(n, e_of[(3, 1)[way]]), r_x.at[n, way])
            f_copy(n, way).start()
            c_copy(n, (3, 1)[way]).start()

    def far_chunk(n):
        for way in range(2):
            landed(chunk(n, e_of[2], 4 * way, 4), r_f.at[n, way])
        c_copy(n, 2).start()

    def rows_arrive():
        def wait_r(d, _):
            ys = rem(y + NY - d, NY)
            o = ys * NZ + zl
            both = div(LIST8 * o, PER_DEV) != div(LIST8 * o + LIST8 - 1, PER_DEV)
            landed(rbuf.at[ys, 0], r_r.at[d, 0])
            pltpu.make_async_copy(rbuf.at[ys, 0], rs.at[ys, 0], l_r.at[d, 0]).start()

            @pl.when(both)
            def _():
                landed(rbuf.at[ys, 1], r_r.at[d, 1])
                pltpu.make_async_copy(rbuf.at[ys, 1], rs.at[ys, 1], l_r.at[d, 1]).start()

            return 0

        lax.fori_loop(0, NY, wait_r, 0)

        def wait_l(d, _):
            ys = rem(y + NY - d, NY)
            o = ys * NZ + zl
            both = div(LIST8 * o, PER_DEV) != div(LIST8 * o + LIST8 - 1, PER_DEV)
            pltpu.make_async_copy(rbuf.at[ys, 0], rs.at[ys, 0], l_r.at[d, 0]).wait()
            pl.when(both)(pltpu.make_async_copy(rbuf.at[ys, 1], rs.at[ys, 1], l_r.at[d, 1]).wait)
            return 0

        lax.fori_loop(0, NY, wait_l, 0)

        def invert(i, _):
            ys, g = div(i, NZ), rem(i, NZ)
            o = ys * NZ + zl
            found = [jnp.int32(ZERO)] * LIST8
            for t in range(LIST8):
                which, lane = place(o, t)
                row = rs[ys, which, g, 0, lane] & 7
                for p in range(RCAP):
                    at = (t // RCAP) * RCAP + p
                    found[at] = jnp.where(row == p, t * 8 + ys, found[at])
            for at in range(LIST8):
                idxs[i * LIST8 + at] = found[at]
            return 0

        lax.fori_loop(0, NY * NZ, invert, 0)

    def multiply(n):
        g = rem(zl + 1 + n, NZ)
        for d in range(NX):
            landed(chunk(n, rem(x + d, NX) * 2 + 1 - k), r_c.at[n, d])

        def wait_b(d, _):
            landed(bbuf.at[n, rem(y + NY - d, NY)], r_b.at[n, d])
            return 0

        lax.fori_loop(1, NY, wait_b, 0)
        acc[...] = jnp.zeros_like(acc)

        def step(ys, _):
            at = (ys * NZ + g) * LIST8
            panel = bbuf[n, ys].reshape(2 * BS, BS)
            left = jnp.concatenate(
                [
                    jnp.concatenate([held[n][idxs[at + p]], held[n][idxs[at + RCAP + p]]], axis=1)
                    for p in range(RCAP)
                ],
                axis=0,
            )
            acc[...] += jnp.dot(left, panel, preferred_element_type=jnp.float32)
            return 0

        lax.fori_loop(0, NY, step, 0)

    def o_copy(n):
        return remote(ostage.at[n], obuf.at[n], s_o.at[n], r_o.at[n], at_z(rem(zl + 1 + n, NZ)))

    def hand_over(n):
        multiply(n)
        ostage[n] = acc[...].astype(jnp.bfloat16)
        o_copy(n).start()

    own_chunk(0)
    send_s2(2)
    rows_arrive()
    own_chunk(1)
    send_s2(3)
    near_chunks(0)
    own_chunk(2)
    far_chunk(0)
    near_chunks(1)
    sent_b(0)
    send_b(3)
    own_chunk(3)
    far_chunk(1)
    hand_over(0)
    near_chunks(2)
    hand_over(1)
    far_chunk(2)
    near_chunks(3)
    hand_over(2)
    far_chunk(3)
    loads[4].wait()
    multiply(3)
    for n in range(3):
        landed(obuf.at[n], r_o.at[n])
    for p in range(RCAP):
        at = pl.ds(p * BS, BS)
        total = acc[at, :]
        for n in range(3):
            total = total + obuf[n, at, :].astype(jnp.float32)
        out_ref[at, :] = (total * mask_ref[p, 0].astype(jnp.float32)).astype(jnp.bfloat16)

    for t in range(3):
        away, _, far, _ = i1(t)
        pl.when(away)(far.wait_send)

    def sent_s1(j, _):
        s = PER_DEV * c + j

        @pl.when((s < USED) & jnp.logical_not(is_self(j)))
        def _():
            remote(a_ref.at[j], a0.at[0], s_s1.at[j], r_s1.at[0, 0], other).wait_send()

        return 0

    lax.fori_loop(0, PER_DEV, sent_s1, 0)

    @pl.when(holds)
    def _():
        def sent(i, _):
            i2(rem(c + i, N_COL)).wait_send()
            return 0

        lax.fori_loop(1, N_COL, sent, 0)

    def sent_y(d, _):
        for n in range(1, 4):
            b_copy(n, d).wait_send()
        r_copy(d, 0).wait_send()
        pl.when(two)(lambda: r_copy(d, 1).wait_send())
        return 0

    lax.fori_loop(1, NY, sent_y, 0)
    for n in range(4):
        for d in (1, 2):
            s2(n, d, 0).wait_send()
            pl.when(three)(lambda n=n, d=d: s2(n, d, 1).wait_send())
        for way in range(2):
            x_copy(n, way).wait_send()
            f_copy(n, way).wait_send()
        for d in range(NX):
            c_copy(n, d).wait_send()
        if n < 3:
            o_copy(n).wait_send()


def per_device(a_vals, a_row, a_col, group_rows, b_panel, c_mask):
    vmem, smem, dma = pltpu.VMEM, pltpu.SMEM, pltpu.SemaphoreType.DMA
    block = (BS, BS)
    bf16, i32 = jnp.bfloat16, jnp.int32
    return pl.pallas_call(
        kernel,
        out_shape=jax.ShapeDtypeStruct((RCAP * BS, BS), bf16),
        in_specs=[pl.BlockSpec(memory_space=pl.ANY)] * 6,
        out_specs=pl.BlockSpec(memory_space=vmem),
        scratch_shapes=[
            vmem((1, PER_DEV), i32),
            vmem((1, PER_DEV), i32),
            smem((1,), i32),
            vmem((KB_DEV,) + block, bf16),
            smem((RCAP, 1), i32),
            dma((5,)),
            *[vmem((ZERO + 1,) + block, bf16)] * 4,
            vmem((4, NY, 2) + block, bf16),
            vmem((4, NY, 2) + block, bf16),
            vmem((1, 128), i32),
            vmem((N_ROW, 1, 128), i32),
            vmem((2, N_ROW, 1, 128), i32),
            smem((2, N_ROW, 1, 128), i32),
            vmem((NY, 2, NZ, 1, 128), i32),
            smem((NY, 2, NZ, 1, 128), i32),
            smem((NY * NZ * LIST8,), i32),
            vmem((3, RCAP * BS, BS), bf16),
            vmem((3, RCAP * BS, BS), bf16),
            vmem((RCAP * BS, BS), jnp.float32),
            dma((3,)), dma((N_ROW,)),
            dma((N_COL,)), dma((2,)), dma((2,)),
            dma((PER_DEV,)), dma((4, NY)),
            dma((4, 2, 2)), dma((4, 2, 2)),
            dma((4, 2)), dma((4, 2)),
            dma((4, 2)), dma((4, 2)),
            dma((4, NX)), dma((4, NX)),
            dma((4, NY)), dma((4, NY)),
            dma((NY, 2)), dma((NY, 2)), dma((NY, 2)),
            dma((3,)), dma((3,)),
        ],
        compiler_params=pltpu.CompilerParams(
            collective_id=0, has_side_effects=True, vmem_limit_bytes=40 << 20
        ),
        cost_estimate=pl.CostEstimate(flops=2 * 256 * BS**3, bytes_accessed=2 << 20, transcendentals=0),
    )(
        a_vals.reshape((PER_DEV,) + block),
        a_row,
        a_col,
        group_rows,
        b_panel.reshape((KB_DEV,) + block),
        c_mask,
    )


def solution(mesh):
    in_specs = (
        P("row", "col", None, None),
        P("row", "col"),
        P("row", "col"),
        P("row"),
        P("row", "col"),
        P("row", "col"),
    )
    return jax.shard_map(
        per_device, mesh=mesh, in_specs=in_specs, out_specs=P("row", "col"), check_vma=False
    )
```

```python
import jax
import jax.numpy as jnp
from jax import lax
from jax.experimental import pallas as pl
from jax.experimental.pallas import tpu as pltpu
from jax.sharding import PartitionSpec as P

BS = 128
RCAP = 4
KB_DEV = 24
PER_DEV = 11
USED = 256
N_ROW = 32
N_COL = 24
NY, NZ, NH, NX = 8, 4, 3, 4
LIST8 = 8
ZERO = 64
MESH = pl.DeviceIdType.MESH


def div(a, b):
    return lax.div(jnp.int32(a), jnp.int32(b))


def rem(a, b):
    return lax.rem(jnp.int32(a), jnp.int32(b))


def owners_in(zl, h):
    first = PER_DEV * h + rem(zl + h, NZ)
    last = jnp.minimum(PER_DEV * h + PER_DEV - 1, N_ROW - 1)
    return div(first, NZ), first + 2 * NZ <= last


def kernel(
    a_ref, row_hbm, col_hbm, live_hbm, b_hbm, mask_hbm, out_ref,
    row_ref, col_ref, live_ref, b_ref, mask_ref, l_in, a0, a1, a2, a3, bbuf, bstage, pk, ix1, ix2, sx, rbuf, rs, idxs, ostage, obuf, acc,
    s_i1, r_i1, s_i2, r_i2, l_i2, s_s1, r_s1, s_s2, r_s2, s_x, r_x, s_f, r_f, s_c, r_c,
    s_b, r_b, s_r, r_r, l_r, s_o, r_o,
):
    held = (a0, a1, a2, a3)
    r = lax.axis_index("row")
    c = lax.axis_index("col")
    y, zl = div(r, NZ), rem(r, NZ)
    h, e = div(c, 8), rem(c, 8)
    x, k = div(e, 2), rem(e, 2)
    ca, cb = div(LIST8 * r, PER_DEV), div(LIST8 * r + LIST8 - 1, PER_DEV)
    two = cb != ca
    holds = (c == ca) | (c == cb)
    slot = jnp.where(c == ca, 0, 1)
    o_lo = div(PER_DEV * c, LIST8)
    o_hi = jnp.minimum(div(PER_DEV * c + PER_DEV - 1, LIST8), N_ROW - 1)

    runs = [owners_in(zl, rem(h + d, NH)) for d in range(NH)]
    y0, three = runs[0]

    def at_h(d):
        return (r, rem(h + d, NH) * 8 + e)

    def at_x(d):
        return (r, h * 8 + rem(x + d, NX) * 2 + k)

    def at_y(d):
        return (rem(y + d, NY) * NZ + zl, c)

    def at_z(z):
        return (y * NZ + z, c)

    other = (r, h * 8 + 2 * x + 1 - k)

    def remote(src, dst, s_sem, r_sem, device):
        return pltpu.make_async_remote_copy(
            src_ref=src, dst_ref=dst, send_sem=s_sem, recv_sem=r_sem,
            device_id=device, device_id_type=MESH,
        )

    loads = [
        pltpu.make_async_copy(src, dst, l_in.at[i])
        for i, (src, dst) in enumerate(
            (
                (row_hbm, row_ref), (col_hbm, col_ref), (live_hbm, live_ref),
                (b_hbm, b_ref), (mask_hbm, mask_ref),
            )
        )
    ]
    for load in loads:
        load.start()

    barrier = pltpu.get_barrier_semaphore()

    def signal(device):
        pl.semaphore_signal(barrier, inc=1, device_id=device, device_id_type=MESH)

    for d in (1, 2):
        signal(at_h(d))
    for d in (1, 3):
        signal(at_x(d))
    signal(other)
    for d in range(1, NY):
        signal(at_y(d))
    for d in range(1, NZ):
        signal(at_z(rem(zl + d, NZ)))

    def greet_s1(i, _):
        g, t = rem(i, NZ), div(i, NZ)
        o = (y0 + t) * NZ + zl
        cs = div(LIST8 * o + e, PER_DEV)
        ok = (t < 2) | three

        @pl.when(ok & ((g != zl) | (cs != c)))
        def _():
            signal((y * NZ + g, cs))

        return 0

    lax.fori_loop(0, 12, greet_s1, 0)

    @pl.when(c != ca)
    def _():
        signal((r, ca))

    @pl.when(two & (c != cb))
    def _():
        signal((r, cb))

    @pl.when(holds)
    def _():
        def greet(i, _):
            signal((rem(r + i, N_ROW), c))
            return 0

        lax.fori_loop(1, N_ROW, greet, 0)

    def is_self(j):
        s = PER_DEV * c + j
        return (rem(div(s, LIST8), NZ) == zl) & (rem(s, LIST8) == e)

    for load in loads[:3]:
        load.wait()
    rows = row_ref[...]
    rows = jnp.where(rows < live_ref[0], rows, RCAP)
    pk[...] = jnp.zeros_like(pk)
    pk[:, 0:PER_DEV] = col_ref[...] * 8 + rows
    for n in range(4):
        held[n][ZERO] = jnp.zeros((BS, BS), jnp.bfloat16)

    expect = jnp.int32(15)
    for j in range(PER_DEV):
        s = PER_DEV * c + j
        expect = expect + jnp.where((s < USED) & jnp.logical_not(is_self(j)), 1, 0)
    for t in range(3):
        expect = expect + jnp.where((o_lo + t <= o_hi) & (o_lo + t != r), 1, 0)
    expect = expect + jnp.where(holds, N_COL - 1, 0)
    pl.semaphore_wait(barrier, expect)

    def i1(t):
        o = o_lo + t
        return (
            (o <= o_hi) & (o != r),
            (o <= o_hi) & (o == r),
            remote(pk, ix1.at[r], s_i1.at[t], r_i1.at[r], (o, c)),
            pltpu.make_async_copy(pk, ix1.at[r], r_i1.at[r]),
        )

    for t in range(3):
        away, here, far, near = i1(t)
        pl.when(away)(far.start)
        pl.when(here)(near.start)

    def send_s1(n):
        zd = rem(zl + 3 - n, NZ)

        def one(j, _):
            s = PER_DEV * c + j
            e2, y2 = rem(s, LIST8), div(s, 4 * LIST8)
            ok = (s < USED) & (rem(div(s, LIST8), NZ) == zd)
            src, dst, sem = a_ref.at[j], held[n].at[e2 * 8 + y2], r_s1.at[n, y2]
            if n == 3:

                @pl.when(ok & (e2 == e))
                def _():
                    pltpu.make_async_copy(src, dst, sem).start()

                ok = ok & (e2 != e)

            @pl.when(ok)
            def _():
                remote(src, dst, s_s1.at[j], sem, (y * NZ + zd, h * 8 + e2)).start()

            return 0

        lax.fori_loop(0, PER_DEV, one, 0)

    send_s1(0)
    send_s1(1)

    def i2(cc):
        return remote(ix1, ix2.at[slot], s_i2.at[cc], r_i2.at[slot], (r, cc))

    @pl.when(holds)
    def _():
        def take(i, _):
            remote(pk, ix1.at[i], s_i1.at[0], r_i1.at[i], other).wait_recv()
            return 0

        lax.fori_loop(0, N_ROW, take, 0)
        pltpu.make_async_copy(ix1, ix2.at[slot], r_i2.at[slot]).start()

        def give(i, _):
            i2(rem(c + i, N_COL)).start()
            return 0

        lax.fori_loop(1, N_COL, give, 0)

    def s2(n, d, part):
        src = held[n].at[pl.ds(e * 8 + y0 + 2 * part, 2 - part)]
        return remote(src, src, s_s2.at[n, d - 1, part], r_s2.at[n, d - 1, part], at_h(d))

    def take_s1(n, t):
        dst = held[n].at[e * 8 + y0 + t]
        remote(dst, dst, s_s1.at[0], r_s1.at[n, y0 + t], other).wait_recv()

    def send_s2(n):
        take_s1(n, 0)
        take_s1(n, 1)
        for d in (1, 2):
            s2(n, d, 0).start()

        @pl.when(three)
        def _():
            take_s1(n, 2)
            for d in (1, 2):
                s2(n, d, 1).start()

    def chunk(n, ec, lo=0, size=8):
        return held[n].at[pl.ds(ec * 8 + lo, size)]

    e_of = [rem(x + d, NX) * 2 + k for d in range(NX)]

    def run(n, ec, d, part):
        return held[n].at[pl.ds(ec * 8 + runs[d][0] + 2 * part, 2 - part)]

    def x_copy(n, way, d, part):
        src = run(n, e, d, part)
        return remote(src, src, s_x.at[n, way, d, part], r_x.at[n, way, d, part], at_x((1, 3)[way]))

    def send_x(n, d):
        x_copy(n, 0, d, 0).start()
        x_copy(n, 1, d, 0).start()

        @pl.when(runs[d][1])
        def _():
            x_copy(n, 0, d, 1).start()
            x_copy(n, 1, d, 1).start()

    def f_copy(n, way):
        src = chunk(n, e_of[(3, 1)[way]], 4 * way, 4)
        return remote(src, src, s_f.at[n, way], r_f.at[n, way], at_x((1, 3)[way]))

    def c_copy(n, d):
        src = chunk(n, e_of[d])
        return remote(src, src, s_c.at[n, d], r_c.at[n, d], other)

    def landed(ref, sem):
        remote(ref, ref, s_c.at[0, 0], sem, other).wait_recv()

    def own_chunk(n):
        for d in (1, 2):
            landed(run(n, e, NH - d, 0), r_s2.at[n, d - 1, 0])

            @pl.when(runs[NH - d][1])
            def _(d=d):
                landed(run(n, e, NH - d, 1), r_s2.at[n, d - 1, 1])

            send_x(n, NH - d)
        c_copy(n, 0).start()

    def near_chunks(n):
        for way in range(2):
            ec = e_of[(3, 1)[way]]
            for d in range(NH):
                landed(run(n, ec, d, 0), r_x.at[n, way, d, 0])

                @pl.when(runs[d][1])
                def _(way=way, ec=ec, d=d):
                    landed(run(n, ec, d, 1), r_x.at[n, way, d, 1])

            f_copy(n, way).start()
            c_copy(n, (3, 1)[way]).start()

    def far_chunk(n):
        for way in range(2):
            landed(chunk(n, e_of[2], 4 * way, 4), r_f.at[n, way])
        c_copy(n, 2).start()

    send_s2(0)
    send_x(0, 0)

    def wait_i2(i):
        remote(ix1, ix2.at[i], s_i2.at[0], r_i2.at[i], other).wait_recv()
        pltpu.make_async_copy(ix2.at[i], sx.at[i], l_i2.at[i]).start()

    wait_i2(0)
    pl.when(two)(lambda: wait_i2(1))
    pltpu.make_async_copy(ix2.at[0], sx.at[0], l_i2.at[0]).wait()
    pl.when(two)(pltpu.make_async_copy(ix2.at[1], sx.at[1], l_i2.at[1]).wait)

    def b_copy(n, d):
        return remote(bstage.at[n, d], bbuf.at[n, y], s_b.at[n, d], r_b.at[n, d], at_y(d))

    def place(o, t):
        s = LIST8 * o + t
        cs = div(s, PER_DEV)
        return jnp.where(cs == div(LIST8 * o, PER_DEV), 0, 1), s - PER_DEV * cs

    def chosen(rr, q):
        which, lane = place(r, RCAP * q)
        return jnp.clip((sx[which, rr, 0, lane] >> 3) - KB_DEV * r, 0, KB_DEV - 1)

    def send_b(n):
        g = rem(zl + 1 + n, NZ)

        def one(i, _):
            d = 1 + rem(3 * i + 3, 7)
            for q in range(2):
                bstage[n, d, q] = b_ref[chosen(rem(y + d, NY) * NZ + g, q)]
            b_copy(n, d).start()
            return 0

        lax.fori_loop(0, NY - 1, one, 0)
        for q in range(2):
            bbuf[n, y, q] = b_ref[chosen(r - zl + g, q)]

    def sent_b(n):
        def one(d, _):
            b_copy(n, d).wait_send()
            return 0

        lax.fori_loop(1, NY, one, 0)

    def r_copy(d, i):
        src = ix2.at[i, pl.ds(rem(y + d, NY) * NZ, NZ)]
        return remote(src, rbuf.at[y, i], s_r.at[d, i], r_r.at[d, i], at_y(d))

    def r_own(i):
        return pltpu.make_async_copy(ix2.at[i, pl.ds(y * NZ, NZ)], rbuf.at[y, i], r_r.at[0, i])

    def send_r():
        def one(d, _):
            r_copy(d, 0).start()
            pl.when(two)(lambda: r_copy(d, 1).start())
            return 0

        lax.fori_loop(1, NY, one, 0)
        r_own(0).start()
        pl.when(two)(lambda: r_own(1).start())

    loads[3].wait()
    send_s1(2)
    send_s1(3)
    send_b(0)
    send_s2(1)
    send_x(1, 0)
    send_r()
    send_b(1)
    send_b(2)

    def rows_arrive():
        def wait_r(d, _):
            ys = rem(y + NY - d, NY)
            o = ys * NZ + zl
            both = div(LIST8 * o, PER_DEV) != div(LIST8 * o + LIST8 - 1, PER_DEV)
            landed(rbuf.at[ys, 0], r_r.at[d, 0])
            pltpu.make_async_copy(rbuf.at[ys, 0], rs.at[ys, 0], l_r.at[d, 0]).start()

            @pl.when(both)
            def _():
                landed(rbuf.at[ys, 1], r_r.at[d, 1])
                pltpu.make_async_copy(rbuf.at[ys, 1], rs.at[ys, 1], l_r.at[d, 1]).start()

            return 0

        lax.fori_loop(0, NY, wait_r, 0)

        def wait_l(d, _):
            ys = rem(y + NY - d, NY)
            o = ys * NZ + zl
            both = div(LIST8 * o, PER_DEV) != div(LIST8 * o + LIST8 - 1, PER_DEV)
            pltpu.make_async_copy(rbuf.at[ys, 0], rs.at[ys, 0], l_r.at[d, 0]).wait()
            pl.when(both)(pltpu.make_async_copy(rbuf.at[ys, 1], rs.at[ys, 1], l_r.at[d, 1]).wait)
            return 0

        lax.fori_loop(0, NY, wait_l, 0)

        def invert(i, _):
            ys, g = div(i, NZ), rem(i, NZ)
            o = ys * NZ + zl
            found = [jnp.int32(ZERO)] * LIST8
            for t in range(LIST8):
                which, lane = place(o, t)
                row = rs[ys, which, g, 0, lane] & 7
                for p in range(RCAP):
                    at = (t // RCAP) * RCAP + p
                    found[at] = jnp.where(row == p, t * 8 + ys, found[at])
            for at in range(LIST8):
                idxs[i * LIST8 + at] = found[at]
            return 0

        lax.fori_loop(0, NY * NZ, invert, 0)

    def multiply(n):
        g = rem(zl + 1 + n, NZ)
        for d in range(NX):
            landed(chunk(n, rem(x + d, NX) * 2 + 1 - k), r_c.at[n, d])

        def wait_b(d, _):
            landed(bbuf.at[n, rem(y + NY - d, NY)], r_b.at[n, d])
            return 0

        lax.fori_loop(1, NY, wait_b, 0)
        acc[...] = jnp.zeros_like(acc)

        def step(ys, _):
            at = (ys * NZ + g) * LIST8
            panel = bbuf[n, ys].reshape(2 * BS, BS)
            left = jnp.concatenate(
                [
                    jnp.concatenate([held[n][idxs[at + p]], held[n][idxs[at + RCAP + p]]], axis=1)
                    for p in range(RCAP)
                ],
                axis=0,
            )
            acc[...] += jnp.dot(left, panel, preferred_element_type=jnp.float32)
            return 0

        lax.fori_loop(0, NY, step, 0)

    def o_copy(n):
        return remote(ostage.at[n], obuf.at[n], s_o.at[n], r_o.at[n], at_z(rem(zl + 1 + n, NZ)))

    def hand_over(n):
        multiply(n)
        ostage[n] = acc[...].astype(jnp.bfloat16)
        o_copy(n).start()

    own_chunk(0)
    send_s2(2)
    send_x(2, 0)
    own_chunk(1)
    send_s2(3)
    send_x(3, 0)
    near_chunks(0)
    rows_arrive()
    own_chunk(2)
    far_chunk(0)
    near_chunks(1)
    sent_b(0)
    send_b(3)
    own_chunk(3)
    far_chunk(1)
    hand_over(0)
    near_chunks(2)
    hand_over(1)
    far_chunk(2)
    near_chunks(3)
    hand_over(2)
    far_chunk(3)
    loads[4].wait()
    multiply(3)
    for n in range(3):
        landed(obuf.at[n], r_o.at[n])
    for p in range(RCAP):
        at = pl.ds(p * BS, BS)
        total = acc[at, :]
        for n in range(3):
            total = total + obuf[n, at, :].astype(jnp.float32)
        out_ref[at, :] = (total * mask_ref[p, 0].astype(jnp.float32)).astype(jnp.bfloat16)

    for t in range(3):
        away, _, far, _ = i1(t)
        pl.when(away)(far.wait_send)

    def sent_s1(j, _):
        s = PER_DEV * c + j

        @pl.when((s < USED) & jnp.logical_not(is_self(j)))
        def _():
            remote(a_ref.at[j], a0.at[0], s_s1.at[j], r_s1.at[0, 0], other).wait_send()

        return 0

    lax.fori_loop(0, PER_DEV, sent_s1, 0)

    @pl.when(holds)
    def _():
        def sent(i, _):
            i2(rem(c + i, N_COL)).wait_send()
            return 0

        lax.fori_loop(1, N_COL, sent, 0)

    def sent_y(d, _):
        for n in range(1, 4):
            b_copy(n, d).wait_send()
        r_copy(d, 0).wait_send()
        pl.when(two)(lambda: r_copy(d, 1).wait_send())
        return 0

    lax.fori_loop(1, NY, sent_y, 0)
    for n in range(4):
        for d in (1, 2):
            s2(n, d, 0).wait_send()
            pl.when(three)(lambda n=n, d=d: s2(n, d, 1).wait_send())
        for way in range(2):
            for d in range(NH):
                x_copy(n, way, d, 0).wait_send()
                pl.when(runs[d][1])(lambda n=n, way=way, d=d: x_copy(n, way, d, 1).wait_send())
            f_copy(n, way).wait_send()
        for d in range(NX):
            c_copy(n, d).wait_send()
        if n < 3:
            o_copy(n).wait_send()


def per_device(a_vals, a_row, a_col, group_rows, b_panel, c_mask):
    vmem, smem, dma = pltpu.VMEM, pltpu.SMEM, pltpu.SemaphoreType.DMA
    block = (BS, BS)
    bf16, i32 = jnp.bfloat16, jnp.int32
    return pl.pallas_call(
        kernel,
        out_shape=jax.ShapeDtypeStruct((RCAP * BS, BS), bf16),
        in_specs=[pl.BlockSpec(memory_space=pl.ANY)] * 6,
        out_specs=pl.BlockSpec(memory_space=vmem),
        scratch_shapes=[
            vmem((1, PER_DEV), i32),
            vmem((1, PER_DEV), i32),
            smem((1,), i32),
            vmem((KB_DEV,) + block, bf16),
            smem((RCAP, 1), i32),
            dma((5,)),
            *[vmem((ZERO + 1,) + block, bf16)] * 4,
            vmem((4, NY, 2) + block, bf16),
            vmem((4, NY, 2) + block, bf16),
            vmem((1, 128), i32),
            vmem((N_ROW, 1, 128), i32),
            vmem((2, N_ROW, 1, 128), i32),
            smem((2, N_ROW, 1, 128), i32),
            vmem((NY, 2, NZ, 1, 128), i32),
            smem((NY, 2, NZ, 1, 128), i32),
            smem((NY * NZ * LIST8,), i32),
            vmem((3, RCAP * BS, BS), bf16),
            vmem((3, RCAP * BS, BS), bf16),
            vmem((RCAP * BS, BS), jnp.float32),
            dma((3,)), dma((N_ROW,)),
            dma((N_COL,)), dma((2,)), dma((2,)),
            dma((PER_DEV,)), dma((4, NY)),
            dma((4, 2, 2)), dma((4, 2, 2)),
            dma((4, 2, NH, 2)), dma((4, 2, NH, 2)),
            dma((4, 2)), dma((4, 2)),
            dma((4, NX)), dma((4, NX)),
            dma((4, NY)), dma((4, NY)),
            dma((NY, 2)), dma((NY, 2)), dma((NY, 2)),
            dma((3,)), dma((3,)),
        ],
        compiler_params=pltpu.CompilerParams(
            collective_id=0, has_side_effects=True, vmem_limit_bytes=40 << 20
        ),
        cost_estimate=pl.CostEstimate(flops=2 * 256 * BS**3, bytes_accessed=2 << 20, transcendentals=0),
    )(
        a_vals.reshape((PER_DEV,) + block),
        a_row,
        a_col,
        group_rows,
        b_panel.reshape((KB_DEV,) + block),
        c_mask,
    )


def solution(mesh):
    in_specs = (
        P("row", "col", None, None),
        P("row", "col"),
        P("row", "col"),
        P("row"),
        P("row", "col"),
        P("row", "col"),
    )
    return jax.shard_map(
        per_device, mesh=mesh, in_specs=in_specs, out_specs=P("row", "col"), check_vma=False
    )
```

```python
import jax
import jax.numpy as jnp
from jax import lax
from jax.experimental import pallas as pl
from jax.experimental.pallas import tpu as pltpu
from jax.sharding import PartitionSpec as P

BS = 128
RCAP = 4
KB_DEV = 24
PER_DEV = 11
USED = 256
N_ROW = 32
N_COL = 24
NY, NZ, NH, NX = 8, 4, 3, 4
LIST8 = 8
ZERO = 64
MESH = pl.DeviceIdType.MESH


def div(a, b):
    return lax.div(jnp.int32(a), jnp.int32(b))


def rem(a, b):
    return lax.rem(jnp.int32(a), jnp.int32(b))


def owners_in(zl, h):
    first = PER_DEV * h + rem(zl + h, NZ)
    last = jnp.minimum(PER_DEV * h + PER_DEV - 1, N_ROW - 1)
    return div(first, NZ), first + 2 * NZ <= last


def kernel(
    a_ref, row_hbm, col_hbm, live_hbm, b_hbm, mask_hbm, out_ref,
    row_ref, col_ref, live_ref, b_ref, mask_ref, l_in, a0, a1, a2, a3, bbuf, bstage, pk, ix1, ix2, sx, rbuf, rs, idxs, ostage, obuf, acc,
    s_i1, r_i1, s_i2, r_i2, l_i2, s_s1, r_s1, s_s2, r_s2, s_x, r_x, s_f, r_f, s_c, r_c,
    s_b, r_b, s_r, r_r, l_r, s_o, r_o,
):
    held = (a0, a1, a2, a3)
    r = lax.axis_index("row")
    c = lax.axis_index("col")
    y, zl = div(r, NZ), rem(r, NZ)
    h, e = div(c, 8), rem(c, 8)
    x, k = div(e, 2), rem(e, 2)
    ca, cb = div(LIST8 * r, PER_DEV), div(LIST8 * r + LIST8 - 1, PER_DEV)
    two = cb != ca
    holds = (c == ca) | (c == cb)
    slot = jnp.where(c == ca, 0, 1)
    o_lo = div(PER_DEV * c, LIST8)
    o_hi = jnp.minimum(div(PER_DEV * c + PER_DEV - 1, LIST8), N_ROW - 1)

    runs = [owners_in(zl, rem(h + d, NH)) for d in range(NH)]
    y0, three = runs[0]

    def at_h(d):
        return (r, rem(h + d, NH) * 8 + e)

    def at_x(d):
        return (r, h * 8 + rem(x + d, NX) * 2 + k)

    def at_y(d):
        return (rem(y + d, NY) * NZ + zl, c)

    def at_z(z):
        return (y * NZ + z, c)

    other = (r, h * 8 + 2 * x + 1 - k)

    def remote(src, dst, s_sem, r_sem, device):
        return pltpu.make_async_remote_copy(
            src_ref=src, dst_ref=dst, send_sem=s_sem, recv_sem=r_sem,
            device_id=device, device_id_type=MESH,
        )

    loads = [
        pltpu.make_async_copy(src, dst, l_in.at[i])
        for i, (src, dst) in enumerate(
            (
                (row_hbm, row_ref), (col_hbm, col_ref), (live_hbm, live_ref),
                (b_hbm, b_ref), (mask_hbm, mask_ref),
            )
        )
    ]
    for load in loads:
        load.start()

    barrier = pltpu.get_barrier_semaphore()

    def signal(device):
        pl.semaphore_signal(barrier, inc=1, device_id=device, device_id_type=MESH)

    for d in (1, 2):
        signal(at_h(d))
    for d in (1, 3):
        signal(at_x(d))
    signal(other)
    for d in range(1, NY):
        signal(at_y(d))
    for d in range(1, NZ):
        signal(at_z(rem(zl + d, NZ)))

    def greet_s1(i, _):
        g, t = rem(i, NZ), div(i, NZ)
        o = (y0 + t) * NZ + zl
        cs = div(LIST8 * o + e, PER_DEV)
        ok = (t < 2) | three

        @pl.when(ok & ((g != zl) | (cs != c)))
        def _():
            signal((y * NZ + g, cs))

        return 0

    lax.fori_loop(0, 12, greet_s1, 0)

    @pl.when(c != ca)
    def _():
        signal((r, ca))

    @pl.when(two & (c != cb))
    def _():
        signal((r, cb))

    @pl.when(holds)
    def _():
        def greet(i, _):
            signal((rem(r + i, N_ROW), c))
            return 0

        lax.fori_loop(1, N_ROW, greet, 0)

    def is_self(j):
        s = PER_DEV * c + j
        return (rem(div(s, LIST8), NZ) == zl) & (rem(s, LIST8) == e)

    for load in loads[:3]:
        load.wait()
    rows = row_ref[...]
    rows = jnp.where(rows < live_ref[0], rows, RCAP)
    pk[...] = jnp.zeros_like(pk)
    pk[:, 0:PER_DEV] = col_ref[...] * 8 + rows
    for n in range(4):
        held[n][ZERO] = jnp.zeros((BS, BS), jnp.bfloat16)

    expect = jnp.int32(15)
    for j in range(PER_DEV):
        s = PER_DEV * c + j
        expect = expect + jnp.where((s < USED) & jnp.logical_not(is_self(j)), 1, 0)
    for t in range(3):
        expect = expect + jnp.where((o_lo + t <= o_hi) & (o_lo + t != r), 1, 0)
    expect = expect + jnp.where(holds, N_COL - 1, 0)
    pl.semaphore_wait(barrier, expect)

    def i1(t):
        o = o_lo + t
        return (
            (o <= o_hi) & (o != r),
            (o <= o_hi) & (o == r),
            remote(pk, ix1.at[r], s_i1.at[t], r_i1.at[r], (o, c)),
            pltpu.make_async_copy(pk, ix1.at[r], r_i1.at[r]),
        )

    for t in range(3):
        away, here, far, near = i1(t)
        pl.when(away)(far.start)
        pl.when(here)(near.start)

    def send_s1(n):
        zd = rem(zl + 3 - n, NZ)

        def one(j, _):
            s = PER_DEV * c + j
            e2, y2 = rem(s, LIST8), div(s, 4 * LIST8)
            ok = (s < USED) & (rem(div(s, LIST8), NZ) == zd)
            src, dst, sem = a_ref.at[j], held[n].at[e2 * 8 + y2], r_s1.at[n, y2]
            if n == 3:

                @pl.when(ok & (e2 == e))
                def _():
                    pltpu.make_async_copy(src, dst, sem).start()

                ok = ok & (e2 != e)

            @pl.when(ok)
            def _():
                remote(src, dst, s_s1.at[j], sem, (y * NZ + zd, h * 8 + e2)).start()

            return 0

        lax.fori_loop(0, PER_DEV, one, 0)

    send_s1(0)
    send_s1(1)

    def i2(cc):
        return remote(ix1, ix2.at[slot], s_i2.at[cc], r_i2.at[slot], (r, cc))

    @pl.when(holds)
    def _():
        def take(i, _):
            remote(pk, ix1.at[i], s_i1.at[0], r_i1.at[i], other).wait_recv()
            return 0

        lax.fori_loop(0, N_ROW, take, 0)
        pltpu.make_async_copy(ix1, ix2.at[slot], r_i2.at[slot]).start()

        def give(i, _):
            i2(rem(c + i, N_COL)).start()
            return 0

        lax.fori_loop(1, N_COL, give, 0)

    def s2(n, d, part):
        src = held[n].at[pl.ds(e * 8 + y0 + 2 * part, 2 - part)]
        return remote(src, src, s_s2.at[n, d - 1, part], r_s2.at[n, d - 1, part], at_h(d))

    def take_s1(n, t):
        dst = held[n].at[e * 8 + y0 + t]
        remote(dst, dst, s_s1.at[0], r_s1.at[n, y0 + t], other).wait_recv()

    def send_s2(n):
        take_s1(n, 0)
        take_s1(n, 1)
        for d in (1, 2):
            s2(n, d, 0).start()

        @pl.when(three)
        def _():
            take_s1(n, 2)
            for d in (1, 2):
                s2(n, d, 1).start()

    def chunk(n, ec, lo=0, size=8):
        return held[n].at[pl.ds(ec * 8 + lo, size)]

    e_of = [rem(x + d, NX) * 2 + k for d in range(NX)]

    def run(n, ec, d, part):
        return held[n].at[pl.ds(ec * 8 + runs[d][0] + 2 * part, 2 - part)]

    def x_copy(n, way, d, part):
        src = run(n, e, d, part)
        return remote(src, src, s_x.at[n, way, d, part], r_x.at[n, way, d, part], at_x((1, 3)[way]))

    def send_x(n, d):
        x_copy(n, 0, d, 0).start()
        x_copy(n, 1, d, 0).start()

        @pl.when(runs[d][1])
        def _():
            x_copy(n, 0, d, 1).start()
            x_copy(n, 1, d, 1).start()

    def f_copy(n, way):
        src = chunk(n, e_of[(3, 1)[way]], 4 * way, 4)
        return remote(src, src, s_f.at[n, way], r_f.at[n, way], at_x((1, 3)[way]))

    def c_copy(n, d):
        src = chunk(n, e_of[d])
        return remote(src, src, s_c.at[n, d], r_c.at[n, d], other)

    def landed(ref, sem):
        remote(ref, ref, s_c.at[0, 0], sem, other).wait_recv()

    def own_chunk(n):
        for d in (1, 2):
            landed(run(n, e, NH - d, 0), r_s2.at[n, d - 1, 0])

            @pl.when(runs[NH - d][1])
            def _(d=d):
                landed(run(n, e, NH - d, 1), r_s2.at[n, d - 1, 1])

            send_x(n, NH - d)
        c_copy(n, 0).start()

    def near_chunks(n):
        for way in range(2):
            ec = e_of[(3, 1)[way]]
            for d in range(NH):
                landed(run(n, ec, d, 0), r_x.at[n, way, d, 0])

                @pl.when(runs[d][1])
                def _(way=way, ec=ec, d=d):
                    landed(run(n, ec, d, 1), r_x.at[n, way, d, 1])

            f_copy(n, way).start()
            c_copy(n, (3, 1)[way]).start()

    def far_chunk(n):
        for way in range(2):
            landed(chunk(n, e_of[2], 4 * way, 4), r_f.at[n, way])
        c_copy(n, 2).start()

    send_s2(0)
    send_x(0, 0)
    send_s2(1)
    send_x(1, 0)
    send_s1(2)
    send_s1(3)

    def wait_i2(i):
        remote(ix1, ix2.at[i], s_i2.at[0], r_i2.at[i], other).wait_recv()
        pltpu.make_async_copy(ix2.at[i], sx.at[i], l_i2.at[i]).start()

    wait_i2(0)
    pl.when(two)(lambda: wait_i2(1))
    pltpu.make_async_copy(ix2.at[0], sx.at[0], l_i2.at[0]).wait()
    pl.when(two)(pltpu.make_async_copy(ix2.at[1], sx.at[1], l_i2.at[1]).wait)

    def b_copy(n, d):
        return remote(bstage.at[n, d], bbuf.at[n, y], s_b.at[n, d], r_b.at[n, d], at_y(d))

    def place(o, t):
        s = LIST8 * o + t
        cs = div(s, PER_DEV)
        return jnp.where(cs == div(LIST8 * o, PER_DEV), 0, 1), s - PER_DEV * cs

    def chosen(rr, q):
        which, lane = place(r, RCAP * q)
        return jnp.clip((sx[which, rr, 0, lane] >> 3) - KB_DEV * r, 0, KB_DEV - 1)

    def send_b(n):
        g = rem(zl + 1 + n, NZ)

        def one(i, _):
            d = 1 + rem(3 * i + 3, 7)
            for q in range(2):
                bstage[n, d, q] = b_ref[chosen(rem(y + d, NY) * NZ + g, q)]
            b_copy(n, d).start()
            return 0

        lax.fori_loop(0, NY - 1, one, 0)
        for q in range(2):
            bbuf[n, y, q] = b_ref[chosen(r - zl + g, q)]

    def sent_b(n):
        def one(d, _):
            b_copy(n, d).wait_send()
            return 0

        lax.fori_loop(1, NY, one, 0)

    def r_copy(d, i):
        src = ix2.at[i, pl.ds(rem(y + d, NY) * NZ, NZ)]
        return remote(src, rbuf.at[y, i], s_r.at[d, i], r_r.at[d, i], at_y(d))

    def r_own(i):
        return pltpu.make_async_copy(ix2.at[i, pl.ds(y * NZ, NZ)], rbuf.at[y, i], r_r.at[0, i])

    def send_r():
        def one(d, _):
            r_copy(d, 0).start()
            pl.when(two)(lambda: r_copy(d, 1).start())
            return 0

        lax.fori_loop(1, NY, one, 0)
        r_own(0).start()
        pl.when(two)(lambda: r_own(1).start())

    loads[3].wait()
    send_b(0)
    send_r()
    send_b(1)
    send_b(2)

    def rows_arrive():
        def wait_r(d, _):
            ys = rem(y + NY - d, NY)
            o = ys * NZ + zl
            both = div(LIST8 * o, PER_DEV) != div(LIST8 * o + LIST8 - 1, PER_DEV)
            landed(rbuf.at[ys, 0], r_r.at[d, 0])
            pltpu.make_async_copy(rbuf.at[ys, 0], rs.at[ys, 0], l_r.at[d, 0]).start()

            @pl.when(both)
            def _():
                landed(rbuf.at[ys, 1], r_r.at[d, 1])
                pltpu.make_async_copy(rbuf.at[ys, 1], rs.at[ys, 1], l_r.at[d, 1]).start()

            return 0

        lax.fori_loop(0, NY, wait_r, 0)

        def wait_l(d, _):
            ys = rem(y + NY - d, NY)
            o = ys * NZ + zl
            both = div(LIST8 * o, PER_DEV) != div(LIST8 * o + LIST8 - 1, PER_DEV)
            pltpu.make_async_copy(rbuf.at[ys, 0], rs.at[ys, 0], l_r.at[d, 0]).wait()
            pl.when(both)(pltpu.make_async_copy(rbuf.at[ys, 1], rs.at[ys, 1], l_r.at[d, 1]).wait)
            return 0

        lax.fori_loop(0, NY, wait_l, 0)

        def invert(i, _):
            ys, g = div(i, NZ), rem(i, NZ)
            o = ys * NZ + zl
            found = [jnp.int32(ZERO)] * LIST8
            for t in range(LIST8):
                which, lane = place(o, t)
                row = rs[ys, which, g, 0, lane] & 7
                for p in range(RCAP):
                    at = (t // RCAP) * RCAP + p
                    found[at] = jnp.where(row == p, t * 8 + ys, found[at])
            for at in range(LIST8):
                idxs[i * LIST8 + at] = found[at]
            return 0

        lax.fori_loop(0, NY * NZ, invert, 0)

    def multiply(n):
        g = rem(zl + 1 + n, NZ)
        for d in range(NX):
            landed(chunk(n, rem(x + d, NX) * 2 + 1 - k), r_c.at[n, d])

        def wait_b(d, _):
            landed(bbuf.at[n, rem(y + NY - d, NY)], r_b.at[n, d])
            return 0

        lax.fori_loop(1, NY, wait_b, 0)
        acc[...] = jnp.zeros_like(acc)

        def step(ys, _):
            at = (ys * NZ + g) * LIST8
            panel = bbuf[n, ys].reshape(2 * BS, BS)
            left = jnp.concatenate(
                [
                    jnp.concatenate([held[n][idxs[at + p]], held[n][idxs[at + RCAP + p]]], axis=1)
                    for p in range(RCAP)
                ],
                axis=0,
            )
            acc[...] += jnp.dot(left, panel, preferred_element_type=jnp.float32)
            return 0

        lax.fori_loop(0, NY, step, 0)

    def o_copy(n):
        return remote(ostage.at[n], obuf.at[n], s_o.at[n], r_o.at[n], at_z(rem(zl + 1 + n, NZ)))

    def hand_over(n):
        multiply(n)
        ostage[n] = acc[...].astype(jnp.bfloat16)
        o_copy(n).start()

    own_chunk(0)
    send_s2(2)
    send_x(2, 0)
    own_chunk(1)
    send_s2(3)
    send_x(3, 0)
    near_chunks(0)
    rows_arrive()
    own_chunk(2)
    far_chunk(0)
    near_chunks(1)
    sent_b(0)
    send_b(3)
    own_chunk(3)
    far_chunk(1)
    hand_over(0)
    near_chunks(2)
    hand_over(1)
    far_chunk(2)
    near_chunks(3)
    hand_over(2)
    far_chunk(3)
    loads[4].wait()
    multiply(3)
    for n in range(3):
        landed(obuf.at[n], r_o.at[n])
    for p in range(RCAP):
        at = pl.ds(p * BS, BS)
        total = acc[at, :]
        for n in range(3):
            total = total + obuf[n, at, :].astype(jnp.float32)
        out_ref[at, :] = (total * mask_ref[p, 0].astype(jnp.float32)).astype(jnp.bfloat16)

    for t in range(3):
        away, _, far, _ = i1(t)
        pl.when(away)(far.wait_send)

    def sent_s1(j, _):
        s = PER_DEV * c + j

        @pl.when((s < USED) & jnp.logical_not(is_self(j)))
        def _():
            remote(a_ref.at[j], a0.at[0], s_s1.at[j], r_s1.at[0, 0], other).wait_send()

        return 0

    lax.fori_loop(0, PER_DEV, sent_s1, 0)

    @pl.when(holds)
    def _():
        def sent(i, _):
            i2(rem(c + i, N_COL)).wait_send()
            return 0

        lax.fori_loop(1, N_COL, sent, 0)

    def sent_y(d, _):
        for n in range(1, 4):
            b_copy(n, d).wait_send()
        r_copy(d, 0).wait_send()
        pl.when(two)(lambda: r_copy(d, 1).wait_send())
        return 0

    lax.fori_loop(1, NY, sent_y, 0)
    for n in range(4):
        for d in (1, 2):
            s2(n, d, 0).wait_send()
            pl.when(three)(lambda n=n, d=d: s2(n, d, 1).wait_send())
        for way in range(2):
            for d in range(NH):
                x_copy(n, way, d, 0).wait_send()
                pl.when(runs[d][1])(lambda n=n, way=way, d=d: x_copy(n, way, d, 1).wait_send())
            f_copy(n, way).wait_send()
        for d in range(NX):
            c_copy(n, d).wait_send()
        if n < 3:
            o_copy(n).wait_send()


def per_device(a_vals, a_row, a_col, group_rows, b_panel, c_mask):
    vmem, smem, dma = pltpu.VMEM, pltpu.SMEM, pltpu.SemaphoreType.DMA
    block = (BS, BS)
    bf16, i32 = jnp.bfloat16, jnp.int32
    return pl.pallas_call(
        kernel,
        out_shape=jax.ShapeDtypeStruct((RCAP * BS, BS), bf16),
        in_specs=[pl.BlockSpec(memory_space=pl.ANY)] * 6,
        out_specs=pl.BlockSpec(memory_space=vmem),
        scratch_shapes=[
            vmem((1, PER_DEV), i32),
            vmem((1, PER_DEV), i32),
            smem((1,), i32),
            vmem((KB_DEV,) + block, bf16),
            smem((RCAP, 1), i32),
            dma((5,)),
            *[vmem((ZERO + 1,) + block, bf16)] * 4,
            vmem((4, NY, 2) + block, bf16),
            vmem((4, NY, 2) + block, bf16),
            vmem((1, 128), i32),
            vmem((N_ROW, 1, 128), i32),
            vmem((2, N_ROW, 1, 128), i32),
            smem((2, N_ROW, 1, 128), i32),
            vmem((NY, 2, NZ, 1, 128), i32),
            smem((NY, 2, NZ, 1, 128), i32),
            smem((NY * NZ * LIST8,), i32),
            vmem((3, RCAP * BS, BS), bf16),
            vmem((3, RCAP * BS, BS), bf16),
            vmem((RCAP * BS, BS), jnp.float32),
            dma((3,)), dma((N_ROW,)),
            dma((N_COL,)), dma((2,)), dma((2,)),
            dma((PER_DEV,)), dma((4, NY)),
            dma((4, 2, 2)), dma((4, 2, 2)),
            dma((4, 2, NH, 2)), dma((4, 2, NH, 2)),
            dma((4, 2)), dma((4, 2)),
            dma((4, NX)), dma((4, NX)),
            dma((4, NY)), dma((4, NY)),
            dma((NY, 2)), dma((NY, 2)), dma((NY, 2)),
            dma((3,)), dma((3,)),
        ],
        compiler_params=pltpu.CompilerParams(
            collective_id=0, has_side_effects=True, vmem_limit_bytes=60 << 20
        ),
        cost_estimate=pl.CostEstimate(flops=2 * 256 * BS**3, bytes_accessed=2 << 20, transcendentals=0),
    )(
        a_vals.reshape((PER_DEV,) + block),
        a_row,
        a_col,
        group_rows,
        b_panel.reshape((KB_DEV,) + block),
        c_mask,
    )


def solution(mesh):
    in_specs = (
        P("row", "col", None, None),
        P("row", "col"),
        P("row", "col"),
        P("row"),
        P("row", "col"),
        P("row", "col"),
    )
    return jax.shard_map(
        per_device, mesh=mesh, in_specs=in_specs, out_specs=P("row", "col"), check_vma=False
    )
```

```python
import jax
import jax.numpy as jnp
from jax import lax
from jax.experimental import pallas as pl
from jax.experimental.pallas import tpu as pltpu
from jax.sharding import PartitionSpec as P

BS = 128
RCAP = 4
KB_DEV = 24
PER_DEV = 11
USED = 256
N_ROW = 32
N_COL = 24
NY, NZ, NH, NX = 8, 4, 3, 4
LIST8 = 8
ZERO = 64
MESH = pl.DeviceIdType.MESH


def div(a, b):
    return lax.div(jnp.int32(a), jnp.int32(b))


def rem(a, b):
    return lax.rem(jnp.int32(a), jnp.int32(b))


def owners_in(zl, h):
    first = PER_DEV * h + rem(zl + h, NZ)
    last = jnp.minimum(PER_DEV * h + PER_DEV - 1, N_ROW - 1)
    return div(first, NZ), first + 2 * NZ <= last


def kernel(
    a_ref, row_hbm, col_hbm, live_hbm, b_hbm, mask_hbm, out_ref,
    row_ref, col_ref, live_ref, b_ref, mask_ref, l_in, a0, a1, a2, a3, bbuf, bstage, pk, ix1, ix2, sx, rbuf, rs, idxs, ostage, obuf, acc,
    s_i1, r_i1, s_i2, r_i2, l_i2, s_s1, r_s1, s_s2, r_s2, s_x, r_x, s_f, r_f, s_c, r_c,
    s_b, r_b, s_r, r_r, l_r, s_o, r_o,
):
    held = (a0, a1, a2, a3)
    r = lax.axis_index("row")
    c = lax.axis_index("col")
    y, zl = div(r, NZ), rem(r, NZ)
    h, e = div(c, 8), rem(c, 8)
    x, k = div(e, 2), rem(e, 2)
    ca, cb = div(LIST8 * r, PER_DEV), div(LIST8 * r + LIST8 - 1, PER_DEV)
    two = cb != ca
    holds = (c == ca) | (c == cb)
    slot = jnp.where(c == ca, 0, 1)
    o_lo = div(PER_DEV * c, LIST8)
    o_hi = jnp.minimum(div(PER_DEV * c + PER_DEV - 1, LIST8), N_ROW - 1)

    runs = [owners_in(zl, rem(h + d, NH)) for d in range(NH)]
    y0, three = runs[0]

    def at_h(d):
        return (r, rem(h + d, NH) * 8 + e)

    def at_x(d):
        return (r, h * 8 + rem(x + d, NX) * 2 + k)

    def at_y(d):
        return (rem(y + d, NY) * NZ + zl, c)

    def at_z(z):
        return (y * NZ + z, c)

    other = (r, h * 8 + 2 * x + 1 - k)

    def remote(src, dst, s_sem, r_sem, device):
        return pltpu.make_async_remote_copy(
            src_ref=src, dst_ref=dst, send_sem=s_sem, recv_sem=r_sem,
            device_id=device, device_id_type=MESH,
        )

    loads = [
        pltpu.make_async_copy(src, dst, l_in.at[i])
        for i, (src, dst) in enumerate(
            (
                (row_hbm, row_ref), (col_hbm, col_ref), (live_hbm, live_ref),
                (b_hbm, b_ref), (mask_hbm, mask_ref),
            )
        )
    ]
    for load in loads:
        load.start()

    barrier = pltpu.get_barrier_semaphore()

    def signal(device):
        pl.semaphore_signal(barrier, inc=1, device_id=device, device_id_type=MESH)

    for d in (1, 2):
        signal(at_h(d))
    for d in (1, 3):
        signal(at_x(d))
    signal(other)
    for d in range(1, NY):
        signal(at_y(d))
    for d in range(1, NZ):
        signal(at_z(rem(zl + d, NZ)))

    def greet_s1(i, _):
        g, t = rem(i, NZ), div(i, NZ)
        o = (y0 + t) * NZ + zl
        cs = div(LIST8 * o + e, PER_DEV)
        ok = (t < 2) | three

        @pl.when(ok & ((g != zl) | (cs != c)))
        def _():
            signal((y * NZ + g, cs))

        return 0

    lax.fori_loop(0, 12, greet_s1, 0)

    @pl.when(c != ca)
    def _():
        signal((r, ca))

    @pl.when(two & (c != cb))
    def _():
        signal((r, cb))

    @pl.when(holds)
    def _():
        def greet(i, _):
            signal((rem(r + i, N_ROW), c))
            return 0

        lax.fori_loop(1, N_ROW, greet, 0)

    def is_self(j):
        s = PER_DEV * c + j
        return (rem(div(s, LIST8), NZ) == zl) & (rem(s, LIST8) == e)

    for load in loads[:3]:
        load.wait()
    rows = row_ref[...]
    rows = jnp.where(rows < live_ref[0], rows, RCAP)
    pk[...] = jnp.zeros_like(pk)
    pk[:, 0:PER_DEV] = col_ref[...] * 8 + rows
    for n in range(4):
        held[n][ZERO] = jnp.zeros((BS, BS), jnp.bfloat16)

    expect = jnp.int32(15)
    for j in range(PER_DEV):
        s = PER_DEV * c + j
        expect = expect + jnp.where((s < USED) & jnp.logical_not(is_self(j)), 1, 0)
    for t in range(3):
        expect = expect + jnp.where((o_lo + t <= o_hi) & (o_lo + t != r), 1, 0)
    expect = expect + jnp.where(holds, N_COL - 1, 0)
    pl.semaphore_wait(barrier, expect)

    def i1(t):
        o = o_lo + t
        return (
            (o <= o_hi) & (o != r),
            (o <= o_hi) & (o == r),
            remote(pk, ix1.at[r], s_i1.at[t], r_i1.at[r], (o, c)),
            pltpu.make_async_copy(pk, ix1.at[r], r_i1.at[r]),
        )

    for t in range(3):
        away, here, far, near = i1(t)
        pl.when(away)(far.start)
        pl.when(here)(near.start)

    def send_s1(n):
        zd = rem(zl + 3 - n, NZ)

        def one(j, _):
            s = PER_DEV * c + j
            e2, y2 = rem(s, LIST8), div(s, 4 * LIST8)
            ok = (s < USED) & (rem(div(s, LIST8), NZ) == zd)
            src, dst, sem = a_ref.at[j], held[n].at[e2 * 8 + y2], r_s1.at[n, y2]
            if n == 3:

                @pl.when(ok & (e2 == e))
                def _():
                    pltpu.make_async_copy(src, dst, sem).start()

                ok = ok & (e2 != e)

            @pl.when(ok)
            def _():
                remote(src, dst, s_s1.at[j], sem, (y * NZ + zd, h * 8 + e2)).start()

            return 0

        lax.fori_loop(0, PER_DEV, one, 0)

    send_s1(0)
    send_s1(1)

    def i2(cc):
        return remote(ix1, ix2.at[slot], s_i2.at[cc], r_i2.at[slot], (r, cc))

    @pl.when(holds)
    def _():
        def take(i, _):
            remote(pk, ix1.at[i], s_i1.at[0], r_i1.at[i], other).wait_recv()
            return 0

        lax.fori_loop(0, N_ROW, take, 0)
        pltpu.make_async_copy(ix1, ix2.at[slot], r_i2.at[slot]).start()

        def give(i, _):
            i2(rem(c + i, N_COL)).start()
            return 0

        lax.fori_loop(1, N_COL, give, 0)

    def s2(n, d, part):
        src = held[n].at[pl.ds(e * 8 + y0 + 2 * part, 2 - part)]
        return remote(src, src, s_s2.at[n, d - 1, part], r_s2.at[n, d - 1, part], at_h(d))

    def take_s1(n, t):
        dst = held[n].at[e * 8 + y0 + t]
        remote(dst, dst, s_s1.at[0], r_s1.at[n, y0 + t], other).wait_recv()

    def send_s2(n):
        take_s1(n, 0)
        take_s1(n, 1)
        for d in (1, 2):
            s2(n, d, 0).start()

        @pl.when(three)
        def _():
            take_s1(n, 2)
            for d in (1, 2):
                s2(n, d, 1).start()

    def chunk(n, ec, lo=0, size=8):
        return held[n].at[pl.ds(ec * 8 + lo, size)]

    e_of = [rem(x + d, NX) * 2 + k for d in range(NX)]

    def run(n, ec, d, part):
        return held[n].at[pl.ds(ec * 8 + runs[d][0] + 2 * part, 2 - part)]

    def x_copy(n, way, d, part):
        src = run(n, e, d, part)
        return remote(src, src, s_x.at[n, way, d, part], r_x.at[n, way, d, part], at_x((1, 3)[way]))

    def send_x(n, d):
        x_copy(n, 0, d, 0).start()
        x_copy(n, 1, d, 0).start()

        @pl.when(runs[d][1])
        def _():
            x_copy(n, 0, d, 1).start()
            x_copy(n, 1, d, 1).start()

    def f_copy(n, way):
        src = chunk(n, e_of[(3, 1)[way]], 4 * way, 4)
        return remote(src, src, s_f.at[n, way], r_f.at[n, way], at_x((1, 3)[way]))

    def c_copy(n, d):
        src = chunk(n, e_of[d])
        return remote(src, src, s_c.at[n, d], r_c.at[n, d], other)

    def landed(ref, sem):
        remote(ref, ref, s_c.at[0, 0], sem, other).wait_recv()

    def own_chunk(n):
        for d in (1, 2):
            landed(run(n, e, NH - d, 0), r_s2.at[n, d - 1, 0])

            @pl.when(runs[NH - d][1])
            def _(d=d):
                landed(run(n, e, NH - d, 1), r_s2.at[n, d - 1, 1])

            send_x(n, NH - d)
        c_copy(n, 0).start()

    def near_chunks(n):
        for way in range(2):
            ec = e_of[(3, 1)[way]]
            for d in range(NH):
                landed(run(n, ec, d, 0), r_x.at[n, way, d, 0])

                @pl.when(runs[d][1])
                def _(way=way, ec=ec, d=d):
                    landed(run(n, ec, d, 1), r_x.at[n, way, d, 1])

            f_copy(n, way).start()
            c_copy(n, (3, 1)[way]).start()

    def far_chunk(n):
        for way in range(2):
            landed(chunk(n, e_of[2], 4 * way, 4), r_f.at[n, way])
        c_copy(n, 2).start()

    send_s2(0)
    send_x(0, 0)
    send_s2(1)
    send_x(1, 0)
    send_s1(2)
    send_s1(3)

    def wait_i2(i):
        remote(ix1, ix2.at[i], s_i2.at[0], r_i2.at[i], other).wait_recv()
        pltpu.make_async_copy(ix2.at[i], sx.at[i], l_i2.at[i]).start()

    wait_i2(0)
    pl.when(two)(lambda: wait_i2(1))
    pltpu.make_async_copy(ix2.at[0], sx.at[0], l_i2.at[0]).wait()
    pl.when(two)(pltpu.make_async_copy(ix2.at[1], sx.at[1], l_i2.at[1]).wait)

    def b_copy(n, d):
        return remote(bstage.at[n, d], bbuf.at[n, y], s_b.at[n, d], r_b.at[n, d], at_y(d))

    def place(o, t):
        s = LIST8 * o + t
        cs = div(s, PER_DEV)
        return jnp.where(cs == div(LIST8 * o, PER_DEV), 0, 1), s - PER_DEV * cs

    def chosen(rr, q):
        which, lane = place(r, RCAP * q)
        return jnp.clip((sx[which, rr, 0, lane] >> 3) - KB_DEV * r, 0, KB_DEV - 1)

    def send_b(n):
        g = rem(zl + 1 + n, NZ)

        def one(i, _):
            d = 1 + rem(3 * i + 3, 7)
            for q in range(2):
                bstage[n, d, q] = b_ref[chosen(rem(y + d, NY) * NZ + g, q)]
            b_copy(n, d).start()
            return 0

        lax.fori_loop(0, NY - 1, one, 0)
        for q in range(2):
            bbuf[n, y, q] = b_ref[chosen(r - zl + g, q)]

    def r_copy(d, i):
        src = ix2.at[i, pl.ds(rem(y + d, NY) * NZ, NZ)]
        return remote(src, rbuf.at[y, i], s_r.at[d, i], r_r.at[d, i], at_y(d))

    def r_own(i):
        return pltpu.make_async_copy(ix2.at[i, pl.ds(y * NZ, NZ)], rbuf.at[y, i], r_r.at[0, i])

    def send_r():
        def one(d, _):
            r_copy(d, 0).start()
            pl.when(two)(lambda: r_copy(d, 1).start())
            return 0

        lax.fori_loop(1, NY, one, 0)
        r_own(0).start()
        pl.when(two)(lambda: r_own(1).start())

    loads[3].wait()
    send_b(0)
    send_r()
    send_b(1)
    send_b(2)
    send_b(3)

    def rows_arrive():
        def wait_r(d, _):
            ys = rem(y + NY - d, NY)
            o = ys * NZ + zl
            both = div(LIST8 * o, PER_DEV) != div(LIST8 * o + LIST8 - 1, PER_DEV)
            landed(rbuf.at[ys, 0], r_r.at[d, 0])
            pltpu.make_async_copy(rbuf.at[ys, 0], rs.at[ys, 0], l_r.at[d, 0]).start()

            @pl.when(both)
            def _():
                landed(rbuf.at[ys, 1], r_r.at[d, 1])
                pltpu.make_async_copy(rbuf.at[ys, 1], rs.at[ys, 1], l_r.at[d, 1]).start()

            return 0

        lax.fori_loop(0, NY, wait_r, 0)

        def wait_l(d, _):
            ys = rem(y + NY - d, NY)
            o = ys * NZ + zl
            both = div(LIST8 * o, PER_DEV) != div(LIST8 * o + LIST8 - 1, PER_DEV)
            pltpu.make_async_copy(rbuf.at[ys, 0], rs.at[ys, 0], l_r.at[d, 0]).wait()
            pl.when(both)(pltpu.make_async_copy(rbuf.at[ys, 1], rs.at[ys, 1], l_r.at[d, 1]).wait)
            return 0

        lax.fori_loop(0, NY, wait_l, 0)

        def invert(i, _):
            ys, g = div(i, NZ), rem(i, NZ)
            o = ys * NZ + zl
            found = [jnp.int32(ZERO)] * LIST8
            for t in range(LIST8):
                which, lane = place(o, t)
                row = rs[ys, which, g, 0, lane] & 7
                for p in range(RCAP):
                    at = (t // RCAP) * RCAP + p
                    found[at] = jnp.where(row == p, t * 8 + ys, found[at])
            for at in range(LIST8):
                idxs[i * LIST8 + at] = found[at]
            return 0

        lax.fori_loop(0, NY * NZ, invert, 0)

    def multiply(n):
        g = rem(zl + 1 + n, NZ)
        for d in range(NX):
            landed(chunk(n, rem(x + d, NX) * 2 + 1 - k), r_c.at[n, d])

        def wait_b(d, _):
            landed(bbuf.at[n, rem(y + NY - d, NY)], r_b.at[n, d])
            return 0

        lax.fori_loop(1, NY, wait_b, 0)
        acc[...] = jnp.zeros_like(acc)

        def step(ys, _):
            at = (ys * NZ + g) * LIST8
            panel = bbuf[n, ys].reshape(2 * BS, BS)
            left = jnp.concatenate(
                [
                    jnp.concatenate([held[n][idxs[at + p]], held[n][idxs[at + RCAP + p]]], axis=1)
                    for p in range(RCAP)
                ],
                axis=0,
            )
            acc[...] += jnp.dot(left, panel, preferred_element_type=jnp.float32)
            return 0

        lax.fori_loop(0, NY, step, 0)

    def o_copy(n):
        return remote(ostage.at[n], obuf.at[n], s_o.at[n], r_o.at[n], at_z(rem(zl + 1 + n, NZ)))

    def hand_over(n):
        multiply(n)
        ostage[n] = acc[...].astype(jnp.bfloat16)
        o_copy(n).start()

    own_chunk(0)
    send_s2(2)
    send_x(2, 0)
    own_chunk(1)
    send_s2(3)
    send_x(3, 0)
    near_chunks(0)
    own_chunk(2)
    far_chunk(0)
    near_chunks(1)
    own_chunk(3)
    far_chunk(1)
    rows_arrive()
    hand_over(0)
    near_chunks(2)
    hand_over(1)
    far_chunk(2)
    near_chunks(3)
    hand_over(2)
    far_chunk(3)
    loads[4].wait()
    multiply(3)
    for n in range(3):
        landed(obuf.at[n], r_o.at[n])
    for p in range(RCAP):
        at = pl.ds(p * BS, BS)
        total = acc[at, :]
        for n in range(3):
            total = total + obuf[n, at, :].astype(jnp.float32)
        out_ref[at, :] = (total * mask_ref[p, 0].astype(jnp.float32)).astype(jnp.bfloat16)

    for t in range(3):
        away, _, far, _ = i1(t)
        pl.when(away)(far.wait_send)

    def sent_s1(j, _):
        s = PER_DEV * c + j

        @pl.when((s < USED) & jnp.logical_not(is_self(j)))
        def _():
            remote(a_ref.at[j], a0.at[0], s_s1.at[j], r_s1.at[0, 0], other).wait_send()

        return 0

    lax.fori_loop(0, PER_DEV, sent_s1, 0)

    @pl.when(holds)
    def _():
        def sent(i, _):
            i2(rem(c + i, N_COL)).wait_send()
            return 0

        lax.fori_loop(1, N_COL, sent, 0)

    def sent_y(d, _):
        for n in range(4):
            b_copy(n, d).wait_send()
        r_copy(d, 0).wait_send()
        pl.when(two)(lambda: r_copy(d, 1).wait_send())
        return 0

    lax.fori_loop(1, NY, sent_y, 0)
    for n in range(4):
        for d in (1, 2):
            s2(n, d, 0).wait_send()
            pl.when(three)(lambda n=n, d=d: s2(n, d, 1).wait_send())
        for way in range(2):
            for d in range(NH):
                x_copy(n, way, d, 0).wait_send()
                pl.when(runs[d][1])(lambda n=n, way=way, d=d: x_copy(n, way, d, 1).wait_send())
            f_copy(n, way).wait_send()
        for d in range(NX):
            c_copy(n, d).wait_send()
        if n < 3:
            o_copy(n).wait_send()


def per_device(a_vals, a_row, a_col, group_rows, b_panel, c_mask):
    vmem, smem, dma = pltpu.VMEM, pltpu.SMEM, pltpu.SemaphoreType.DMA
    block = (BS, BS)
    bf16, i32 = jnp.bfloat16, jnp.int32
    return pl.pallas_call(
        kernel,
        out_shape=jax.ShapeDtypeStruct((RCAP * BS, BS), bf16),
        in_specs=[pl.BlockSpec(memory_space=pl.ANY)] * 6,
        out_specs=pl.BlockSpec(memory_space=vmem),
        scratch_shapes=[
            vmem((1, PER_DEV), i32),
            vmem((1, PER_DEV), i32),
            smem((1,), i32),
            vmem((KB_DEV,) + block, bf16),
            smem((RCAP, 1), i32),
            dma((5,)),
            *[vmem((ZERO + 1,) + block, bf16)] * 4,
            vmem((4, NY, 2) + block, bf16),
            vmem((4, NY, 2) + block, bf16),
            vmem((1, 128), i32),
            vmem((N_ROW, 1, 128), i32),
            vmem((2, N_ROW, 1, 128), i32),
            smem((2, N_ROW, 1, 128), i32),
            vmem((NY, 2, NZ, 1, 128), i32),
            smem((NY, 2, NZ, 1, 128), i32),
            smem((NY * NZ * LIST8,), i32),
            vmem((3, RCAP * BS, BS), bf16),
            vmem((3, RCAP * BS, BS), bf16),
            vmem((RCAP * BS, BS), jnp.float32),
            dma((3,)), dma((N_ROW,)),
            dma((N_COL,)), dma((2,)), dma((2,)),
            dma((PER_DEV,)), dma((4, NY)),
            dma((4, 2, 2)), dma((4, 2, 2)),
            dma((4, 2, NH, 2)), dma((4, 2, NH, 2)),
            dma((4, 2)), dma((4, 2)),
            dma((4, NX)), dma((4, NX)),
            dma((4, NY)), dma((4, NY)),
            dma((NY, 2)), dma((NY, 2)), dma((NY, 2)),
            dma((3,)), dma((3,)),
        ],
        compiler_params=pltpu.CompilerParams(
            collective_id=0, has_side_effects=True, vmem_limit_bytes=60 << 20
        ),
        cost_estimate=pl.CostEstimate(flops=2 * 256 * BS**3, bytes_accessed=2 << 20, transcendentals=0),
    )(
        a_vals.reshape((PER_DEV,) + block),
        a_row,
        a_col,
        group_rows,
        b_panel.reshape((KB_DEV,) + block),
        c_mask,
    )


def solution(mesh):
    in_specs = (
        P("row", "col", None, None),
        P("row", "col"),
        P("row", "col"),
        P("row"),
        P("row", "col"),
        P("row", "col"),
    )
    return jax.shard_map(
        per_device, mesh=mesh, in_specs=in_specs, out_specs=P("row", "col"), check_vma=False
    )
```
